128 devices in a mesh: outer: 4 (over x_lo, core), vocab: 32 (over y, z, x_hi).
Axes of the slice: x: 4 (x_hi: 2, x_lo: 2; x = x_hi * 2 + x_lo), y: 4, z: 4, core: 2. Of those that a mesh axis runs over, the one named last changes fastest.
Arguments:
- hidden: bfloat16 [2048, 4096], P(('outer', 'vocab')), parts along dimension 0, may hold values from -96 to 96
- targets: int32 [2048], P(('outer', 'vocab')), parts along dimension 0, may hold values from 0 to 65535
- head: bfloat16 [16384, 65536], P('outer', 'vocab'), parts along dimension 0, may hold values from -1 to 1
- global_frag: float32 [128, 65536], P(None, 'vocab'), may hold values from -6 to 6
- momentum: float32 [128, 65536], P(None, 'vocab'), may hold values from -6 to 6
- peer_delta: float32 [512, 65536], P('outer', 'vocab'), parts along dimension 0, may hold values from -6 to 6
Outputs:
- loss: float32 [4], P('outer'), parts along dimension 0
- hidden_grad: bfloat16 [2048, 4096], P(('outer', 'vocab')), parts along dimension 0
- new_global: float32 [512, 65536], P('outer', 'vocab'), parts along dimension 0
- new_momentum: float32 [512, 65536], P('outer', 'vocab'), parts along dimension 0
The draws below stay inside these ranges and needn't reach their ends.
There are 4 independent parts, one for each index of `outer`. The reference program is written for one: setup_inputs(seed, part) draws one part's arguments, and reference() takes and returns one part's arrays. A program takes and returns all parts, laid end to end along the dimension named above; an argument that names none is the same for every part. Nothing has to cross between parts.
All inputs are finite; a program needn't handle non-finite values.
Results may differ from the reference program's by a relative error of at most 0.0031.
Values may be sent and summed in bfloat16 or wider, within the bound.
A program may use at most 128 MiB of HBM per device.

```python
import jax
import jax.numpy as jnp
from jax import lax

D = 4096
FRAG = 128
REPLICAS = 4
ROWS = 512
VOCAB = 65536


def head_base(key):
    inner = jax.random.fold_in(key, 11)
    values = jnp.clip(jax.random.normal(inner, (D, VOCAB), jnp.float32), -6.0, 6.0)
    return values * D ** (-0.5)


def draw_head(key, part):
    base = head_base(key)
    return base.astype(jnp.bfloat16)


def draw_hidden(key, part):
    key = jax.random.fold_in(key, 3)
    rows_drawn = 3.0 * jnp.clip(jax.random.normal(key, (ROWS, D), jnp.float32), -5.0, 5.0)
    return rows_drawn.astype(jnp.bfloat16)


def plant(result, own_key, low, largest):
    longest = result.shape.index(max(result.shape))
    spots = []
    for shift in (0, 1):
        where = [jax.random.randint(jax.random.fold_in(own_key, axis), (), 0, length) for axis, length in enumerate(result.shape)]
        where[longest] = (where[longest] + shift) % result.shape[longest]
        spots.append(tuple(where))
    return result.at[spots[0]].set(low).at[spots[1]].set(largest)


def levels(stream_key, extent, shards, low, largest):
    def one(axis_at, shards_of):
        steps = jax.random.uniform(jax.random.fold_in(jax.random.fold_in(stream_key, 6), axis_at), (shards_of,), jnp.float32, low / len(shards), largest / len(shards))
        return jnp.repeat(jnp.exp(steps), extent[axis_at] // shards_of).reshape((-1,) + (1,) * (len(extent) - axis_at - 1))

    level = one(*shards[0])
    for cut in shards[1:]:
        level = level * one(*cut)
    return level


def centred(stream_key, extent, scale, bound, pieces=(), held_as=jnp.bfloat16):
    drawn = jax.random.normal(stream_key, extent, jnp.float32) * scale
    if len(pieces) > 0:
        drawn = levels(stream_key, extent, pieces, -0.22, 0.18) * drawn
    return jnp.clip(drawn, min=-bound, max=bound).astype(held_as)


def setup_inputs(seed: int = 0, part: int = 0) -> dict:
    splits = jax.random.split(jax.random.key(seed), 7)
    part_keys = jax.random.split(jax.random.fold_in(splits[6], part), 7)
    return {
        "hidden": draw_hidden(jax.random.fold_in(jax.random.fold_in(splits[6], part), 71), part),
        "targets": plant(jax.random.randint(part_keys[1], (ROWS,), 0, VOCAB), jax.random.fold_in(part_keys[1], 1), 0, VOCAB - 1).astype(jnp.int32),
        "head": draw_head(jax.random.fold_in(jax.random.fold_in(splits[6], part), 71), part),
        "global_frag": centred(splits[3], (FRAG, VOCAB), 1.0, 6.0, ((1, 32),), jnp.float32),
        "momentum": centred(splits[4], (FRAG, VOCAB), 1.0, 6.0, ((1, 32),), jnp.float32),
        "peer_delta": centred(part_keys[5], (FRAG, VOCAB), 1.0, 6.0, ((1, 32),), jnp.float32),
    }


def reference(hidden, targets, head, global_frag, momentum, peer_delta):
    logits = jnp.dot(hidden, head, preferred_element_type=jnp.float32)
    top = jnp.max(logits, axis=1)
    shifted = jnp.exp(logits - top[:, None])
    total = jnp.sum(shifted, axis=1)
    columns = jnp.arange(logits.shape[1], dtype=jnp.int32)
    onehot = (columns[None, :] == targets[:, None]).astype(jnp.float32)
    picked = jnp.sum(logits * onehot, axis=1)
    loss = jnp.mean(top + jnp.log(total) - picked).reshape((1,))
    dlogits = ((shifted / total[:, None] - onehot) / ROWS).astype(jnp.bfloat16)
    hidden_grad = lax.dot_general(dlogits, head, (((1,), (1,)), ((), ())), preferred_element_type=jnp.float32).astype(jnp.bfloat16)
    frag_grad = lax.dot_general(hidden[:, :FRAG], dlogits, (((0,), (0,)), ((), ())), preferred_element_type=jnp.float32)
    local_frag = head[:FRAG].astype(jnp.float32) - 1.0 * frag_grad
    pseudo = (global_frag - local_frag + peer_delta) / REPLICAS
    new_momentum = 0.9 * momentum + pseudo
    new_global = global_frag - 0.7 * (pseudo + 0.9 * new_momentum)
    return loss, hidden_grad, new_global, new_momentum
```

```python
import functools

import jax
import jax.numpy as jnp
from jax import lax
from jax.experimental import pallas as pl
from jax.experimental.pallas import tpu as pltpu
from jax.sharding import PartitionSpec as P

FRAG = 128
REPLICAS = 4
MESH = pl.DeviceIdType.MESH
F32, BF16 = jnp.float32, jnp.bfloat16

NY, NZ, NX = 4, 4, 2
OWN = 16
HALF = NY * NZ * OWN
CHUNK = 1024
EXT = 128
TILE = 512
ORDER = (0, 2, 1, 3)


def kernel(
    hidden_hbm, ext_hbm, head_hbm, global_hbm, momentum_hbm, peer_hbm,
    loss_ref, grad_ref, new_global_hbm, new_momentum_hbm,
    head, g_buf, logits, dl, part, send1, recv1, send2, recv2, summed, recv_a, send_x, recv_x,
    st_y, st_z, st_x, fin, col_top, col_sum, col_pick, fg, mo, pe,
    load_sem, head_sem, frag_sem, out_sem, x_sem, a_sem, b1_sem, b2_sem, st_sem, r1_sem, r2_sem, ra_sem, rx_sem,
):
    outer = lax.axis_index("outer")
    me = lax.axis_index("vocab")
    y, z, xh = me // (NZ * NX), (me // NX) % NZ, me % NX
    width = head.shape[1]
    base = me * width

    def dev(dy=0, dz=0, dx=0):
        return (outer, ((y + dy) % NY) * (NZ * NX) + ((z + dz) % NZ) * NX + (xh + dx) % NX)

    def dev_a(g, d):
        return dev(dy=d) if g == 0 else dev(dz=d)

    def dev_b(g, d):
        return dev(dz=d) if g == 0 else dev(dy=d)

    def at(g, a, b):
        return (a, b) if g == 0 else (b, a)

    def pos(g):
        return (y, z) if g == 0 else (z, y)

    def remote(src, dst, sems, device):
        return pltpu.make_async_remote_copy(
            src_ref=src, dst_ref=dst, send_sem=sems.at[0], recv_sem=sems.at[1], device_id=device, device_id_type=MESH
        )

    sent = []

    def go(copies):
        for copy in copies:
            copy.start()
            sent.append(copy)
        return copies

    def arrived(copies):
        for copy in copies:
            copy.wait_recv()

    loads = [
        pltpu.make_async_copy(hidden_hbm, g_buf.at[xh, y, z, :, pl.ds(0, 4 * CHUNK)], load_sem.at[0]),
        pltpu.make_async_copy(ext_hbm, g_buf.at[xh, y, z, :, pl.ds(4 * CHUNK, EXT)], load_sem.at[1]),
    ]
    for copy in loads:
        copy.start()
    head_loads = {}
    for c in ORDER:
        rows = pl.ds(c * CHUNK, CHUNK)
        head_loads[c] = pltpu.make_async_copy(head_hbm.at[rows], head.at[rows], head_sem.at[c])
        head_loads[c].start()
    frag_loads = [
        pltpu.make_async_copy(src, dst, frag_sem.at[i])
        for i, (src, dst) in enumerate(((global_hbm, fg), (momentum_hbm, mo), (peer_hbm, pe)))
    ]
    for copy in frag_loads:
        copy.start()

    barrier = pltpu.get_barrier_semaphore()
    partners = [dev(dy=1), dev(dy=2), dev(dy=3), dev(dz=1), dev(dz=2), dev(dz=3), dev(dx=1)]
    for partner in partners:
        pl.semaphore_signal(barrier, inc=1, device_id=partner, device_id_type=MESH)
    pl.semaphore_wait(barrier, len(partners))

    def columns(c):
        return pl.ds(c * CHUNK, CHUNK + (EXT if c == 3 else 0))

    for copy in loads:
        copy.wait()
    swap = go([remote(g_buf.at[xh, y, z], g_buf.at[xh, y, z], x_sem, dev(dx=1))])

    def gather_a(h):
        copies = []
        for g in range(2):
            cols = pl.ds(2 * CHUNK * g, 2 * CHUNK + (EXT if g == 1 else 0))
            block = g_buf.at[h, y, z, :, cols]
            copies += [remote(block, block, a_sem.at[h, g, d - 1], dev_a(g, d)) for d in (1, 2, 3)]
        return go(copies)

    def gather_b1(h, c):
        g = c // 2
        b = pos(g)[1]
        block = g_buf.at[(h, *at(g, slice(None), b), slice(None), columns(c))]
        return go([remote(block, block, b1_sem.at[h, c, i], dev_b(g, d)) for i, d in enumerate((1, 3))])

    def gather_b2(h, c, first):
        g = c // 2
        b = pos(g)[1]
        copies = []
        for i, d in enumerate((1, 3)):
            first[i].wait_recv()
            block = g_buf.at[(h, *at(g, slice(2 * i, 2 * i + 2), (b + 4 - d) % 4), slice(None), columns(c))]
            copies += go([remote(block, block, b2_sem.at[h, c, i], dev_b(g, d))])
        return copies

    def forward(h, c, second):
        arrived(second)
        if h == 0:
            head_loads[c].wait()
        lo = c * CHUNK

        @pl.loop(0, width // TILE)
        def _(j):
            cols = pl.ds(pl.multiple_of(j * TILE, TILE), TILE)
            rows = g_buf[h, :, :, :, lo : lo + CHUNK].reshape(HALF, CHUNK)
            out = jnp.dot(rows, head[lo : lo + CHUNK, cols], preferred_element_type=F32)
            if c == ORDER[0]:
                logits[h, :, cols] = out
            else:
                logits[h, :, cols] = logits[h, :, cols] + out

    eye = lax.broadcasted_iota(jnp.int32, (128, 128), 0) == lax.broadcasted_iota(jnp.int32, (128, 128), 1)

    def to_lanes(ref, i):
        return jnp.sum(jnp.where(eye, ref[128 * i : 128 * (i + 1), :], 0.0), axis=0, keepdims=True)

    STEP = 32

    def target_columns(h, i):
        t = g_buf[h, i // 2, pl.ds((i % 2) * 2, 2), :, 4 * CHUNK : 4 * CHUNK + EXT]
        t = t.reshape(STEP, EXT).astype(F32)
        return (t[:, 0:1] * 256.0 + t[:, 1:2]).astype(jnp.int32) - base

    def softmax_local(h):
        @pl.loop(0, HALF // STEP)
        def _(i):
            rows = pl.ds(pl.multiple_of(i * STEP, STEP), STEP)
            values = logits[h, rows, :]
            target = target_columns(h, i)
            column = lax.broadcasted_iota(jnp.int32, (STEP, width), 1)
            top = jnp.max(values, axis=1, keepdims=True)
            shifted = jnp.exp(values - top)
            logits[h, rows, :] = shifted
            col_top[h, rows, :] = jnp.broadcast_to(top, (STEP, 128))
            col_sum[rows, :] = jnp.broadcast_to(jnp.sum(shifted, axis=1, keepdims=True), (STEP, 128))
            picked = jnp.sum(jnp.where(column == target, values, 0.0), axis=1, keepdims=True)
            col_pick[rows, :] = jnp.broadcast_to(picked, (STEP, 128))

    def stat_send(h, stage):
        if stage == 0:
            slot = st_y.at[h, y]
            copies = [remote(slot, slot, st_sem.at[h, d - 1], dev(dy=d)) for d in (1, 2, 3)]
        elif stage == 1:
            slot = st_z.at[h, z]
            copies = [remote(slot, slot, st_sem.at[h, 2 + d], dev(dz=d)) for d in (1, 2, 3)]
        else:
            slot = st_x.at[h, xh]
            copies = [remote(slot, slot, st_sem.at[h, 6], dev(dx=1))]
        return go(copies)

    def stats_start(h):
        tile = [to_lanes(col_top.at[h], i) for i in range(2)]
        tile += [to_lanes(ref, i) for ref in (col_sum, col_pick) for i in range(2)]
        tile += [jnp.zeros((2, 128), F32)]
        st_y[h, y] = jnp.concatenate(tile, axis=0)
        return stat_send(h, 0)

    def combine(ref, h, n):
        tops = [ref[h, i, 0:2, :] for i in range(n)]
        top = functools.reduce(jnp.maximum, tops)
        total = sum(ref[h, i, 2:4, :] * jnp.exp(tops[i] - top) for i in range(n))
        picked = sum(ref[h, i, 4:6, :] for i in range(n))
        return jnp.concatenate([top, total, picked, jnp.zeros((2, 128), F32)], axis=0)

    def stats_next(h, stage, copies):
        arrived(copies)
        if stage == 1:
            st_z[h, z] = combine(st_y, h, NY)
        else:
            st_x[h, xh] = combine(st_z, h, NZ)
        return stat_send(h, stage)

    def stats_end(h, copies):
        arrived(copies)
        fin[h] = combine(st_x, h, NX)

    def gradient_logits(h):
        row_count = NX * HALF
        for i in range(2):
            top = jnp.broadcast_to(fin[h, i : i + 1, :], (128, 128))
            total = jnp.broadcast_to(fin[h, 2 + i : 3 + i, :], (128, 128))
            top = jnp.sum(jnp.where(eye, top, 0.0), axis=1, keepdims=True)
            total = jnp.sum(jnp.where(eye, total, 0.0), axis=1, keepdims=True)
            scale = jnp.exp(col_top[h, 128 * i : 128 * (i + 1), :] - top) / (total * row_count)
            col_sum[128 * i : 128 * (i + 1), :] = scale

        @pl.loop(0, HALF // STEP)
        def _(i):
            rows = pl.ds(pl.multiple_of(i * STEP, STEP), STEP)
            target = target_columns(h, i)
            column = lax.broadcasted_iota(jnp.int32, (STEP, width), 1)
            scale = col_sum[rows, 0:1]
            onehot = jnp.where(column == target, 1.0 / row_count, 0.0)
            dl[h, rows, :] = (logits[h, rows, :] * scale - onehot).astype(BF16)

    def piece(k):
        h, c = k // 4, ORDER[k % 4]
        g = c // 2
        a, b = pos(g)
        return h, c, g, a, b

    def backward(k):
        h, c, g, a, b = piece(k)

        @pl.loop(0, CHUNK // TILE)
        def _(j):
            rows = pl.ds(pl.multiple_of(c * CHUNK + j * TILE, TILE), TILE)
            cols = pl.ds(pl.multiple_of(j * TILE, TILE), TILE)
            out = lax.dot_general(dl[h], head[rows, :], (((1,), (1,)), ((), ())), preferred_element_type=F32)
            part[k, :, :, :, cols] = out.reshape(NY, NZ, OWN, TILE)

        def own(d, first):
            return part[(k, *at(g, slice(first, first + 2), (b + d) % 4))]

        send1[k, 0, 0:2] = own(2, 0).astype(BF16)
        send1[k, 0, 2:4] = own(1, 2).astype(BF16)
        send1[k, 1, 0:2] = own(3, 0).astype(BF16)
        send1[k, 1, 2:4] = own(2, 2).astype(BF16)
        return go(
            [remote(send1.at[k, i], recv1.at[k, i], r1_sem.at[k, i], dev_b(g, d)) for i, d in enumerate((1, 3))]
        )

    def reduce_b(k, first):
        h, c, g, a, b = piece(k)
        copies = []
        for i, d in enumerate((1, 3)):
            first[i].wait_recv()
            mine = part[(k, *at(g, slice(2 * i, 2 * i + 2), (b + d) % 4))]
            send2[k, i] = (mine + recv1[k, i, 2 * i : 2 * i + 2].astype(F32)).astype(BF16)
            copies += go([remote(send2.at[k, i], recv2.at[k, i], r2_sem.at[k, i], dev_b(g, d))])
        return copies

    def reduce_a(k, second):
        h, c, g, a, b = piece(k)
        arrived(second)
        for i in range(2):
            mine = part[(k, *at(g, slice(2 * i, 2 * i + 2), b))]
            near = recv1[k, 1 - i, 2 * i : 2 * i + 2].astype(F32)
            summed[k, 2 * i : 2 * i + 2] = mine + near + recv2[k, i].astype(F32)
        return go(
            [
                remote(summed.at[k, (a + d) % 4], recv_a.at[k, d - 1], ra_sem.at[k, d - 1], dev_a(g, d))
                for d in (1, 2, 3)
            ]
        )

    def reduce_x(k, copies):
        h, c, g, a, b = piece(k)
        arrived(copies)
        send_x[k] = summed[k, a] + recv_a[k, 0] + recv_a[k, 1] + recv_a[k, 2]
        copy = remote(send_x.at[k], recv_x.at[k % 4], rx_sem.at[k % 4], dev(dx=1))

        @pl.when(xh != h)
        def _():
            copy.start()

    def finish():
        for k in range(8):
            h, c, g, a, b = piece(k)
            copy = remote(send_x.at[k], recv_x.at[k % 4], rx_sem.at[k % 4], dev(dx=1))

            @pl.when(xh != h)
            def _():
                copy.wait_send()

            @pl.when(xh == h)
            def _():
                copy.wait_recv()
                grad_ref[:, c * CHUNK : (c + 1) * CHUNK] = (send_x[k] + recv_x[k % 4]).astype(BF16)

    def fragment():
        for copy in frag_loads:
            copy.wait()
        rows = g_buf[:, :, :, :, 0:FRAG].reshape(NX * HALF, FRAG)
        turned = rows.astype(F32).T.astype(BF16)

        @pl.loop(0, width // TILE)
        def _(j):
            cols = pl.ds(pl.multiple_of(j * TILE, TILE), TILE)
            grad = sum(
                jnp.dot(turned[:, h * HALF : (h + 1) * HALF], dl[h, :, cols], preferred_element_type=F32)
                for h in range(NX)
            )
            local = head[0:FRAG, cols].astype(F32) - 1.0 * grad
            outer_value = fg[:, cols]
            pseudo = (outer_value - local + pe[:, cols]) / REPLICAS
            momentum = 0.9 * mo[:, cols] + pseudo
            mo[:, cols] = momentum
            fg[:, cols] = outer_value - 0.7 * (pseudo + 0.9 * momentum)

        stores = [
            pltpu.make_async_copy(fg, new_global_hbm, out_sem.at[0]),
            pltpu.make_async_copy(mo, new_momentum_hbm, out_sem.at[1]),
        ]
        for copy in stores:
            copy.start()
        return stores

    def loss():
        terms = sum(fin[h, 0:2, :] + jnp.log(fin[h, 2:4, :]) - fin[h, 4:6, :] for h in range(NX))
        loss_ref[0] = jnp.sum(terms) / (NX * HALF)

    arrived(swap)
    a0 = gather_a(0)
    arrived(a0)
    b1 = {(0, c): gather_b1(0, c) for c in ORDER[:2]}
    a1 = gather_a(1)
    b1.update({(0, c): gather_b1(0, c) for c in ORDER[2:]})
    b2 = {(0, c): gather_b2(0, c, b1[0, c]) for c in ORDER[:2]}
    arrived(a1)
    b1.update({(1, c): gather_b1(1, c) for c in ORDER[:2]})
    b2.update({(0, c): gather_b2(0, c, b1[0, c]) for c in ORDER[2:]})
    forward(0, 0, b2[0, 0])
    b1.update({(1, c): gather_b1(1, c) for c in ORDER[2:]})
    forward(0, 2, b2[0, 2])
    b2.update({(1, c): gather_b2(1, c, b1[1, c]) for c in ORDER[:2]})
    forward(0, 1, b2[0, 1])
    forward(0, 3, b2[0, 3])
    softmax_local(0)
    s = stats_start(0)
    b2.update({(1, c): gather_b2(1, c, b1[1, c]) for c in ORDER[2:]})
    forward(1, 0, b2[1, 0])
    s = stats_next(0, 1, s)
    forward(1, 2, b2[1, 2])
    s = stats_next(0, 2, s)
    forward(1, 1, b2[1, 1])
    stats_end(0, s)
    gradient_logits(0)
    r = {0: backward(0)}
    forward(1, 3, b2[1, 3])
    r[1] = backward(1)
    r[0] = reduce_b(0, r[0])
    softmax_local(1)
    s = stats_start(1)
    r[1] = reduce_b(1, r[1])
    r[0] = reduce_a(0, r[0])
    r[2] = backward(2)
    s = stats_next(1, 1, s)
    r[1] = reduce_a(1, r[1])
    reduce_x(0, r[0])
    r[2] = reduce_b(2, r[2])
    r[3] = backward(3)
    s = stats_next(1, 2, s)
    reduce_x(1, r[1])
    r[3] = reduce_b(3, r[3])
    r[2] = reduce_a(2, r[2])
    stats_end(1, s)
    gradient_logits(1)
    r[4] = backward(4)
    r[3] = reduce_a(3, r[3])
    reduce_x(2, r[2])
    r[5] = backward(5)
    r[4] = reduce_b(4, r[4])
    reduce_x(3, r[3])
    r[6] = backward(6)
    r[5] = reduce_b(5, r[5])
    r[4] = reduce_a(4, r[4])
    r[7] = backward(7)
    r[6] = reduce_b(6, r[6])
    r[5] = reduce_a(5, r[5])
    reduce_x(4, r[4])
    stores = fragment()
    loss()
    r[7] = reduce_b(7, r[7])
    r[6] = reduce_a(6, r[6])
    reduce_x(5, r[5])
    r[7] = reduce_a(7, r[7])
    reduce_x(6, r[6])
    reduce_x(7, r[7])
    finish()
    for copy in sent:
        copy.wait_send()
    for copy in stores:
        copy.wait()


def body(hidden, targets, head, global_frag, momentum, peer_delta):
    own, depth = hidden.shape
    width = head.shape[1]
    digits = jnp.stack([targets // 256, targets % 256], axis=1).astype(BF16)
    ext = jnp.pad(digits, ((0, 0), (0, EXT - 2)))
    dma = pltpu.SemaphoreType.DMA
    pieces = 8
    loss, grad, new_global, new_momentum = pl.pallas_call(
        kernel,
        out_shape=(
            jax.ShapeDtypeStruct((1,), F32),
            jax.ShapeDtypeStruct((own, depth), BF16),
            jax.ShapeDtypeStruct((FRAG, width), F32),
            jax.ShapeDtypeStruct((FRAG, width), F32),
        ),
        in_specs=[pl.BlockSpec(memory_space=pl.ANY)] * 6,
        out_specs=(
            pl.BlockSpec(memory_space=pltpu.SMEM),
            pl.BlockSpec(memory_space=pltpu.VMEM),
            pl.BlockSpec(memory_space=pl.ANY),
            pl.BlockSpec(memory_space=pl.ANY),
        ),
        scratch_shapes=[
            pltpu.VMEM((depth, width), BF16),
            pltpu.VMEM((NX, NY, NZ, OWN, depth + EXT), BF16),
            pltpu.VMEM((NX, HALF, width), F32),
            pltpu.VMEM((NX, HALF, width), BF16),
            pltpu.VMEM((pieces, NY, NZ, OWN, CHUNK), F32),
            pltpu.VMEM((pieces, 2, 4, OWN, CHUNK), BF16),
            pltpu.VMEM((pieces, 2, 4, OWN, CHUNK), BF16),
            pltpu.VMEM((pieces, 2, 2, OWN, CHUNK), BF16),
            pltpu.VMEM((pieces, 2, 2, OWN, CHUNK), BF16),
            pltpu.VMEM((pieces, 4, OWN, CHUNK), F32),
            pltpu.VMEM((pieces, 3, OWN, CHUNK), F32),
            pltpu.VMEM((pieces, OWN, CHUNK), F32),
            pltpu.VMEM((4, OWN, CHUNK), F32),
            pltpu.VMEM((NX, NY, 8, 128), F32),
            pltpu.VMEM((NX, NZ, 8, 128), F32),
            pltpu.VMEM((NX, NX, 8, 128), F32),
            pltpu.VMEM((NX, 8, 128), F32),
            pltpu.VMEM((NX, HALF, 128), F32),
            pltpu.VMEM((HALF, 128), F32),
            pltpu.VMEM((HALF, 128), F32),
            pltpu.VMEM((FRAG, width), F32),
            pltpu.VMEM((FRAG, width), F32),
            pltpu.VMEM((FRAG, width), F32),
            dma((2,)),
            dma((4,)),
            dma((3,)),
            dma((2,)),
            dma((2,)),
            dma((2, 2, 3, 2)),
            dma((2, 4, 2, 2)),
            dma((2, 4, 2, 2)),
            dma((2, 7, 2)),
            dma((pieces, 2, 2)),
            dma((pieces, 2, 2)),
            dma((pieces, 3, 2)),
            dma((4, 2)),
        ],
        compiler_params=pltpu.CompilerParams(
            collective_id=0, has_side_effects=True, vmem_limit_bytes=62 << 20
        ),
        cost_estimate=pl.CostEstimate(flops=18 * 10**9, bytes_accessed=24 * 2**20, transcendentals=2**20),
    )(hidden, ext, head, global_frag, momentum, peer_delta)
    return loss, grad, new_global, new_momentum


def solution(mesh):
    in_specs = (
        P(("outer", "vocab"), None),
        P(("outer", "vocab")),
        P("outer", "vocab"),
        P(None, "vocab"),
        P(None, "vocab"),
        P("outer", "vocab"),
    )
    out_specs = (P("outer"), P(("outer", "vocab"), None), P("outer", "vocab"), P("outer", "vocab"))
    return jax.shard_map(body, mesh=mesh, in_specs=in_specs, out_specs=out_specs, check_vma=False)
```

```python
import functools

import jax
import jax.numpy as jnp
from jax import lax
from jax.experimental import pallas as pl
from jax.experimental.pallas import tpu as pltpu
from jax.sharding import PartitionSpec as P

FRAG = 128
REPLICAS = 4
MESH = pl.DeviceIdType.MESH
F32, BF16 = jnp.float32, jnp.bfloat16

NY, NZ, NX = 4, 4, 2
OWN = 16
HALF = NY * NZ * OWN
CHUNK = 1024
EXT = 128
TILE = 512
PARTS = 4
ORDER = (0, 2, 1, 3)


def kernel(
    targets_ref, hidden_hbm, head_hbm, global_hbm, momentum_hbm, peer_hbm,
    loss_ref, grad_ref, new_global_hbm, new_momentum_hbm,
    head, g_buf, logits, dl, part, send1, recv1, send2, recv2, summed, recv_a, send_x, recv_x,
    st_plane, st_z, fin, col_top, col_sum, col_pick, fg, mo, pe,
    load_sem, head_sem, frag_sem, out_sem, x_sem, a_sem, b1_sem, b2_sem, st_sem, r1_sem, r2_sem, ra_sem, rx_sem,
):
    outer = lax.axis_index("outer")
    me = lax.axis_index("vocab")
    y, z, xh = me // (NZ * NX), (me // NX) % NZ, me % NX
    width = head.shape[1]
    base = me * width

    def dev(dy=0, dz=0, dx=0):
        return (outer, ((y + dy) % NY) * (NZ * NX) + ((z + dz) % NZ) * NX + (xh + dx) % NX)

    def dev_a(g, d):
        return dev(dy=d) if g == 0 else dev(dz=d)

    def dev_b(g, d):
        return dev(dz=d) if g == 0 else dev(dy=d)

    def at(g, a, b):
        return (a, b) if g == 0 else (b, a)

    def pos(g):
        return (y, z) if g == 0 else (z, y)

    def remote(src, dst, sems, device):
        return pltpu.make_async_remote_copy(
            src_ref=src, dst_ref=dst, send_sem=sems.at[0], recv_sem=sems.at[1], device_id=device, device_id_type=MESH
        )

    sent = []

    def go(copies):
        for copy in copies:
            copy.start()
            sent.append(copy)
        return copies

    def arrived(copies):
        for copy in copies:
            copy.wait_recv()

    load = pltpu.make_async_copy(hidden_hbm, g_buf.at[xh, y, z, :, pl.ds(0, 4 * CHUNK)], load_sem)
    load.start()
    head_loads = {}
    for c in ORDER:
        rows = pl.ds(c * CHUNK, CHUNK)
        head_loads[c] = pltpu.make_async_copy(head_hbm.at[rows], head.at[rows], head_sem.at[c])
        head_loads[c].start()
    frag_loads = [
        pltpu.make_async_copy(src, dst, frag_sem.at[i])
        for i, (src, dst) in enumerate(((global_hbm, fg), (momentum_hbm, mo), (peer_hbm, pe)))
    ]
    for copy in frag_loads:
        copy.start()

    barrier = pltpu.get_barrier_semaphore()
    plane = [(dx, dy) for dx in range(NX) for dy in range(NY) if dx or dy]
    partners = [dev(dz=d) for d in (1, 2, 3)] + [dev(dx=dx, dy=dy) for dx, dy in plane]
    for partner in partners:
        pl.semaphore_signal(barrier, inc=1, device_id=partner, device_id_type=MESH)

    row = lax.broadcasted_iota(jnp.int32, (OWN, EXT), 0)
    lane = lax.broadcasted_iota(jnp.int32, (OWN, EXT), 1)
    digits = jnp.zeros((OWN, EXT), jnp.int32)
    for i in range(OWN):
        target = targets_ref[i]
        digits = jnp.where(row == i, jnp.where(lane == 0, target >> 8, target & 255), digits)
    g_buf[xh, y, z, :, 4 * CHUNK : 4 * CHUNK + EXT] = digits.astype(F32).astype(BF16)
    pl.semaphore_wait(barrier, len(partners))

    def columns(c):
        return pl.ds(c * CHUNK, CHUNK + (EXT if c == 3 else 0))

    load.wait()

    def swap_x(c):
        block = g_buf.at[xh, y, z, :, columns(c)]
        return go([remote(block, block, x_sem.at[c], dev(dx=1))])

    def gather_a(h, c):
        block = g_buf.at[h, y, z, :, columns(c)]
        return [remote(block, block, a_sem.at[h, c, d - 1], dev_a(c // 2, d)) for d in (1, 2, 3)]

    def gather_b1(h, c):
        g = c // 2
        b = pos(g)[1]
        copies = [[None, None], [None, None]]
        for p in range(2):
            for i, d in enumerate((1, 3)):
                q = p if i == 0 else 1 - p
                block = g_buf.at[(h, *at(g, slice(2 * q, 2 * q + 2), b), slice(None), columns(c))]
                (copies[i][q],) = go([remote(block, block, b1_sem.at[h, c, i, q], dev_b(g, d))])
        return copies

    def gather_b2(h, c, first):
        g = c // 2
        b = pos(g)[1]
        copies = []
        for i, d in enumerate((1, 3)):
            first[i][i].wait_recv()
            block = g_buf.at[(h, *at(g, slice(2 * i, 2 * i + 2), (b + 4 - d) % 4), slice(None), columns(c))]
            copies += go([remote(block, block, b2_sem.at[h, c, i], dev_b(g, d))])
        return copies + [first[0][1], first[1][0]]

    def forward(h, c, second):
        arrived(second)
        if h == 0:
            head_loads[c].wait()
        lo = c * CHUNK
        rows = g_buf[h, :, :, :, lo : lo + CHUNK].reshape(HALF, CHUNK)
        out = jnp.dot(rows, head[lo : lo + CHUNK, :], preferred_element_type=F32)
        if c == ORDER[0]:
            logits[h] = out
        else:
            logits[h] = logits[h] + out

    eye = lax.broadcasted_iota(jnp.int32, (128, 128), 0) == lax.broadcasted_iota(jnp.int32, (128, 128), 1)

    def to_lanes(ref, i):
        return jnp.sum(jnp.where(eye, ref[128 * i : 128 * (i + 1), :], 0.0), axis=0, keepdims=True)

    STEP = 32

    def target_columns(h, i):
        t = g_buf[h, i // 2, pl.ds((i % 2) * 2, 2), :, 4 * CHUNK : 4 * CHUNK + EXT]
        t = t.reshape(STEP, EXT).astype(F32)
        return (t[:, 0:1] * 256.0 + t[:, 1:2]).astype(jnp.int32) - base

    def softmax_local(h):
        @pl.loop(0, HALF // STEP)
        def _(i):
            rows = pl.ds(pl.multiple_of(i * STEP, STEP), STEP)
            values = logits[h, rows, :]
            target = target_columns(h, i)
            column = lax.broadcasted_iota(jnp.int32, (STEP, width), 1)
            top = jnp.max(values, axis=1, keepdims=True)
            shifted = jnp.exp(values - top)
            logits[h, rows, :] = shifted
            col_top[h, rows, :] = jnp.broadcast_to(top, (STEP, 128))
            col_sum[rows, :] = jnp.broadcast_to(jnp.sum(shifted, axis=1, keepdims=True), (STEP, 128))
            picked = jnp.sum(jnp.where(column == target, values, 0.0), axis=1, keepdims=True)
            col_pick[rows, :] = jnp.broadcast_to(picked, (STEP, 128))

    def stat_send(h, stage):
        if stage == 0:
            slot = st_plane.at[h, xh, y]
            copies = [remote(slot, slot, st_sem.at[h, dx * NY + dy - 1], dev(dx=dx, dy=dy)) for dx, dy in plane]
        else:
            slot = st_z.at[h, z]
            copies = [remote(slot, slot, st_sem.at[h, 6 + d], dev(dz=d)) for d in (1, 2, 3)]
        return go(copies)

    def stats_start(h):
        tile = [to_lanes(col_top.at[h], i) for i in range(2)]
        tile += [to_lanes(ref, i) for ref in (col_sum, col_pick) for i in range(2)]
        tile += [jnp.zeros((2, 128), F32)]
        st_plane[h, xh, y] = jnp.concatenate(tile, axis=0)
        return stat_send(h, 0)

    def combine(tiles):
        tops = [tile[0:2] for tile in tiles]
        top = functools.reduce(jnp.maximum, tops)
        total = sum(tile[2:4] * jnp.exp(tile[0:2] - top) for tile in tiles)
        picked = sum(tile[4:6] for tile in tiles)
        return jnp.concatenate([top, total, picked, jnp.zeros((2, 128), F32)], axis=0)

    def stats_next(h, copies):
        arrived(copies)
        st_z[h, z] = combine([st_plane[h, i, j] for i in range(NX) for j in range(NY)])
        return stat_send(h, 1)

    def stats_end(h, copies):
        arrived(copies)
        fin[h] = combine([st_z[h, i] for i in range(NZ)])

    def gradient_logits(h):
        row_count = NX * HALF
        for i in range(2):
            top = jnp.broadcast_to(fin[h, i : i + 1, :], (128, 128))
            total = jnp.broadcast_to(fin[h, 2 + i : 3 + i, :], (128, 128))
            top = jnp.sum(jnp.where(eye, top, 0.0), axis=1, keepdims=True)
            total = jnp.sum(jnp.where(eye, total, 0.0), axis=1, keepdims=True)
            scale = jnp.exp(col_top[h, 128 * i : 128 * (i + 1), :] - top) / (total * row_count)
            col_sum[128 * i : 128 * (i + 1), :] = scale

        @pl.loop(0, HALF // STEP)
        def _(i):
            rows = pl.ds(pl.multiple_of(i * STEP, STEP), STEP)
            target = target_columns(h, i)
            column = lax.broadcasted_iota(jnp.int32, (STEP, width), 1)
            scale = col_sum[rows, 0:1]
            onehot = jnp.where(column == target, 1.0 / row_count, 0.0)
            dl[h, rows, :] = (logits[h, rows, :] * scale - onehot).astype(BF16)

    def piece(k):
        h, c = k // 4, ORDER[k % 4]
        g = c // 2
        a, b = pos(g)
        return h, c, g, a, b

    def backward(k):
        h, c, g, a, b = piece(k)

        out = lax.dot_general(
            dl[h], head[c * CHUNK : (c + 1) * CHUNK, :], (((1,), (1,)), ((), ())), preferred_element_type=F32
        )
        part[k] = out.reshape(NY, NZ, OWN, CHUNK)

        def own(d, first):
            return part[(k, *at(g, slice(first, first + 2), (b + d) % 4))]

        send1[k, 0, 0:2] = own(2, 0).astype(BF16)
        send1[k, 1, 2:4] = own(2, 2).astype(BF16)
        copies = [[None, None], [None, None]]
        for p in range(2):
            if p == 1:
                send1[k, 0, 2:4] = own(1, 2).astype(BF16)
                send1[k, 1, 0:2] = own(3, 0).astype(BF16)
            for i, d in enumerate((1, 3)):
                q = p if i == 0 else 1 - p
                half = pl.ds(2 * q, 2)
                (copies[i][q],) = go(
                    [remote(send1.at[k, i, half], recv1.at[k, i, half], r1_sem.at[k, i, q], dev_b(g, d))]
                )
        return copies

    def reduce_b(k, first):
        h, c, g, a, b = piece(k)
        copies = []
        for i, d in enumerate((1, 3)):
            first[i][i].wait_recv()
            mine = part[(k, *at(g, slice(2 * i, 2 * i + 2), (b + d) % 4))]
            send2[k, i] = (mine + recv1[k, i, 2 * i : 2 * i + 2].astype(F32)).astype(BF16)
            copies += go([remote(send2.at[k, i], recv2.at[k, i], r2_sem.at[k, i], dev_b(g, d))])
        return copies + [first[0][1], first[1][0]]

    def reduce_a(k, second):
        h, c, g, a, b = piece(k)
        arrived(second)
        for i in range(2):
            mine = part[(k, *at(g, slice(2 * i, 2 * i + 2), b))]
            near = recv1[k, 1 - i, 2 * i : 2 * i + 2].astype(F32)
            summed[k, 2 * i : 2 * i + 2] = mine + near + recv2[k, i].astype(F32)
        return go(
            [
                remote(summed.at[k, (a + d) % 4], recv_a.at[k, d - 1], ra_sem.at[k, d - 1], dev_a(g, d))
                for d in (1, 2, 3)
            ]
        )

    def reduce_x(k, copies):
        h, c, g, a, b = piece(k)
        arrived(copies)
        send_x[k] = summed[k, a] + recv_a[k, 0] + recv_a[k, 1] + recv_a[k, 2]
        copy = remote(send_x.at[k], recv_x.at[k % 4], rx_sem.at[k % 4], dev(dx=1))

        @pl.when(xh != h)
        def _():
            copy.start()

    def finish():
        for k in range(8):
            h, c, g, a, b = piece(k)
            copy = remote(send_x.at[k], recv_x.at[k % 4], rx_sem.at[k % 4], dev(dx=1))

            @pl.when(xh != h)
            def _():
                copy.wait_send()

            @pl.when(xh == h)
            def _():
                copy.wait_recv()
                grad_ref[:, c * CHUNK : (c + 1) * CHUNK] = (send_x[k] + recv_x[k % 4]).astype(BF16)

    def fragment():
        for copy in frag_loads:
            copy.wait()
        rows = g_buf[:, :, :, :, 0:FRAG].reshape(NX * HALF, FRAG)
        turned = rows.astype(F32).T.astype(BF16)

        @pl.loop(0, width // TILE)
        def _(j):
            cols = pl.ds(pl.multiple_of(j * TILE, TILE), TILE)
            grad = sum(
                jnp.dot(turned[:, h * HALF : (h + 1) * HALF], dl[h, :, cols], preferred_element_type=F32)
                for h in range(NX)
            )
            local = head[0:FRAG, cols].astype(F32) - 1.0 * grad
            outer_value = fg[:, cols]
            pseudo = (outer_value - local + pe[:, cols]) / REPLICAS
            momentum = 0.9 * mo[:, cols] + pseudo
            mo[:, cols] = momentum
            fg[:, cols] = outer_value - 0.7 * (pseudo + 0.9 * momentum)

        stores = [
            pltpu.make_async_copy(fg, new_global_hbm, out_sem.at[0]),
            pltpu.make_async_copy(mo, new_momentum_hbm, out_sem.at[1]),
        ]
        for copy in stores:
            copy.start()
        return stores

    def loss():
        terms = sum(fin[h, 0:2, :] + jnp.log(fin[h, 2:4, :]) - fin[h, 4:6, :] for h in range(NX))
        loss_ref[0] = jnp.sum(terms) / (NX * HALF)

    C0, C1, C2, C3 = ORDER
    xs = {c: swap_x(c) for c in ORDER}
    go(gather_a(xh, C0) + gather_a(xh, C1))
    for c in (C0, C1): arrived(xs[c]); go(gather_a(1 - xh, c))
    b1 = {}
    b2 = {}
    for c in (C0, C1): arrived(gather_a(0, c)); b1[0, c] = gather_b1(0, c)
    go(gather_a(xh, C2) + gather_a(xh, C3))
    for c in (C2, C3): arrived(xs[c]); go(gather_a(1 - xh, c))
    for c in (C0, C1): b2[0, c] = gather_b2(0, c, b1[0, c])
    for c in (C2, C3): arrived(gather_a(0, c)); b1[0, c] = gather_b1(0, c)
    forward(0, C0, b2[0, C0])
    for c in (C0, C1): arrived(gather_a(1, c)); b1[1, c] = gather_b1(1, c)
    for c in (C2, C3): b2[0, c] = gather_b2(0, c, b1[0, c])
    forward(0, C1, b2[0, C1])
    for c in (C2, C3): arrived(gather_a(1, c)); b1[1, c] = gather_b1(1, c)
    for c in (C0, C1): b2[1, c] = gather_b2(1, c, b1[1, c])
    forward(0, C2, b2[0, C2])
    forward(0, C3, b2[0, C3])
    softmax_local(0)
    s = stats_start(0)
    for c in (C2, C3): b2[1, c] = gather_b2(1, c, b1[1, c])
    forward(1, C0, b2[1, C0])
    forward(1, C1, b2[1, C1])
    s = stats_next(0, s)
    forward(1, C2, b2[1, C2])
    stats_end(0, s)
    gradient_logits(0)
    r = {0: backward(0)}
    forward(1, C3, b2[1, C3])
    r[1] = backward(1)
    softmax_local(1)
    s = stats_start(1)
    r[0] = reduce_b(0, r[0])
    r[2] = backward(2)
    r[1] = reduce_b(1, r[1])
    s = stats_next(1, s)
    r[0] = reduce_a(0, r[0])
    r[3] = backward(3)
    r[2] = reduce_b(2, r[2])
    r[1] = reduce_a(1, r[1])
    stats_end(1, s)
    gradient_logits(1)
    r[4] = backward(4)
    r[3] = reduce_b(3, r[3])
    reduce_x(0, r[0])
    r[2] = reduce_a(2, r[2])
    r[5] = backward(5)
    r[4] = reduce_b(4, r[4])
    reduce_x(1, r[1])
    r[3] = reduce_a(3, r[3])
    r[6] = backward(6)
    r[5] = reduce_b(5, r[5])
    reduce_x(2, r[2])
    r[4] = reduce_a(4, r[4])
    r[7] = backward(7)
    r[6] = reduce_b(6, r[6])
    reduce_x(3, r[3])
    r[5] = reduce_a(5, r[5])
    stores = fragment()
    loss()
    r[7] = reduce_b(7, r[7])
    r[6] = reduce_a(6, r[6])
    reduce_x(4, r[4])
    reduce_x(5, r[5])
    r[7] = reduce_a(7, r[7])
    reduce_x(6, r[6])
    reduce_x(7, r[7])
    finish()
    for copy in sent:
        copy.wait_send()
    for copy in stores:
        copy.wait()


def hand_over(loss_in, grad_in, global_in, momentum_in, loss_out, grad_out, global_out, momentum_out):
    loss_out[0] = loss_in[0]
    grad_out[...] = grad_in[...]
    global_out[...] = global_in[...]
    momentum_out[...] = momentum_in[...]


def body(hidden, targets, head, global_frag, momentum, peer_delta):
    own, depth = hidden.shape
    width = head.shape[1]
    dma = pltpu.SemaphoreType.DMA
    pieces = 8
    out_shape = (
        jax.ShapeDtypeStruct((1,), F32),
        jax.ShapeDtypeStruct((own, depth), BF16),
        jax.ShapeDtypeStruct((FRAG, width), F32),
        jax.ShapeDtypeStruct((FRAG, width), F32),
    )
    results = pl.pallas_call(
        kernel,
        out_shape=out_shape,
        in_specs=[pl.BlockSpec(memory_space=pltpu.SMEM)] + [pl.BlockSpec(memory_space=pl.ANY)] * 5,
        out_specs=(
            pl.BlockSpec(memory_space=pltpu.SMEM),
            pl.BlockSpec(memory_space=pltpu.VMEM),
            pl.BlockSpec(memory_space=pl.ANY),
            pl.BlockSpec(memory_space=pl.ANY),
        ),
        scratch_shapes=[
            pltpu.VMEM((depth, width), BF16),
            pltpu.VMEM((NX, NY, NZ, OWN, depth + EXT), BF16),
            pltpu.VMEM((NX, HALF, width), F32),
            pltpu.VMEM((NX, HALF, width), BF16),
            pltpu.VMEM((pieces, NY, NZ, OWN, CHUNK), F32),
            pltpu.VMEM((pieces, 2, 4, OWN, CHUNK), BF16),
            pltpu.VMEM((pieces, 2, 4, OWN, CHUNK), BF16),
            pltpu.VMEM((pieces, 2, 2, OWN, CHUNK), BF16),
            pltpu.VMEM((pieces, 2, 2, OWN, CHUNK), BF16),
            pltpu.VMEM((pieces, 4, OWN, CHUNK), F32),
            pltpu.VMEM((pieces, 3, OWN, CHUNK), F32),
            pltpu.VMEM((pieces, OWN, CHUNK), F32),
            pltpu.VMEM((4, OWN, CHUNK), F32),
            pltpu.VMEM((NX, NX, NY, 8, 128), F32),
            pltpu.VMEM((NX, NZ, 8, 128), F32),
            pltpu.VMEM((NX, 8, 128), F32),
            pltpu.VMEM((NX, HALF, 128), F32),
            pltpu.VMEM((HALF, 128), F32),
            pltpu.VMEM((HALF, 128), F32),
            pltpu.VMEM((FRAG, width), F32),
            pltpu.VMEM((FRAG, width), F32),
            pltpu.VMEM((FRAG, width), F32),
            dma(()),
            dma((4,)),
            dma((3,)),
            dma((2,)),
            dma((4, 2)),
            dma((2, 4, 3, 2)),
            dma((2, 4, 2, 2, 2)),
            dma((2, 4, 2, 2)),
            dma((2, 10, 2)),
            dma((pieces, 2, 2, 2)),
            dma((pieces, 2, 2)),
            dma((pieces, 3, 2)),
            dma((4, 2)),
        ],
        compiler_params=pltpu.CompilerParams(
            collective_id=0, has_side_effects=True, vmem_limit_bytes=62 << 20
        ),
        cost_estimate=pl.CostEstimate(flops=18 * 10**9, bytes_accessed=24 * 2**20, transcendentals=2**20),
    )(targets, hidden, head, global_frag, momentum, peer_delta)
    scalar = pl.BlockSpec(memory_space=pltpu.SMEM)
    grad_block = pl.BlockSpec((own, depth // PARTS), lambda i: (0, i))
    frag_block = pl.BlockSpec((FRAG // PARTS, width), lambda i: (i, 0))
    specs = (scalar, grad_block, frag_block, frag_block)
    return pl.pallas_call(
        hand_over, out_shape=out_shape, grid=(PARTS,), in_specs=specs, out_specs=specs
    )(*results)


def solution(mesh):
    in_specs = (
        P(("outer", "vocab"), None),
        P(("outer", "vocab")),
        P("outer", "vocab"),
        P(None, "vocab"),
        P(None, "vocab"),
        P("outer", "vocab"),
    )
    out_specs = (P("outer"), P(("outer", "vocab"), None), P("outer", "vocab"), P("outer", "vocab"))
    return jax.shard_map(body, mesh=mesh, in_specs=in_specs, out_specs=out_specs, check_vma=False)
```

```python
import functools

import jax
import jax.numpy as jnp
from jax import lax
from jax.experimental import pallas as pl
from jax.experimental.pallas import tpu as pltpu
from jax.sharding import PartitionSpec as P

FRAG = 128
REPLICAS = 4
MESH = pl.DeviceIdType.MESH
F32, BF16 = jnp.float32, jnp.bfloat16

NY, NZ, NX = 4, 4, 2
OWN = 16
HALF = NY * NZ * OWN
CHUNK = 1024
EXT = 128
TILE = 512
PARTS = 4
ORDER = (0, 2, 1, 3)


def kernel(
    targets_ref, hidden_hbm, head_hbm, global_hbm, momentum_hbm, peer_hbm,
    loss_ref, grad_ref, new_global_hbm, new_momentum_hbm,
    head, g_buf, logits, dl, part, send1, recv1, send2, recv2, summed, recv_a, send_x, recv_x,
    st_plane, st_z, fin, col_top, col_sum, col_pick, fg, mo, pe,
    load_sem, head_sem, frag_sem, out_sem, x_sem, a_sem, b1_sem, b2_sem, st_sem, r1_sem, r2_sem, ra_sem, rx_sem,
):
    outer = lax.axis_index("outer")
    me = lax.axis_index("vocab")
    y, z, xh = me // (NZ * NX), (me // NX) % NZ, me % NX
    width = head.shape[1]
    base = me * width

    def dev(dy=0, dz=0, dx=0):
        return (outer, ((y + dy) % NY) * (NZ * NX) + ((z + dz) % NZ) * NX + (xh + dx) % NX)

    def dev_a(g, d):
        return dev(dy=d) if g == 0 else dev(dz=d)

    def dev_b(g, d):
        return dev(dz=d) if g == 0 else dev(dy=d)

    def at(g, a, b):
        return (a, b) if g == 0 else (b, a)

    def pos(g):
        return (y, z) if g == 0 else (z, y)

    def remote(src, dst, sems, device):
        return pltpu.make_async_remote_copy(
            src_ref=src, dst_ref=dst, send_sem=sems.at[0], recv_sem=sems.at[1], device_id=device, device_id_type=MESH
        )

    sent = []

    def go(copies):
        for copy in copies:
            copy.start()
            sent.append(copy)
        return copies

    def arrived(copies):
        for copy in copies:
            copy.wait_recv()

    barrier = pltpu.get_barrier_semaphore()
    plane = [(dx, dy) for dx in range(NX) for dy in range(NY) if dx or dy]
    partners = [dev(dz=d) for d in (1, 2, 3)] + [dev(dx=dx, dy=dy) for dx, dy in plane]
    for partner in partners:
        pl.semaphore_signal(barrier, inc=1, device_id=partner, device_id_type=MESH)

    load = pltpu.make_async_copy(hidden_hbm, g_buf.at[xh, y, z, :, pl.ds(0, 4 * CHUNK)], load_sem)
    load.start()
    head_loads = {}
    for c in ORDER:
        rows = pl.ds(c * CHUNK, CHUNK)
        head_loads[c] = pltpu.make_async_copy(head_hbm.at[rows], head.at[rows], head_sem.at[c])
        head_loads[c].start()
    frag_loads = [
        pltpu.make_async_copy(src, dst, frag_sem.at[i])
        for i, (src, dst) in enumerate(((global_hbm, fg), (momentum_hbm, mo), (peer_hbm, pe)))
    ]
    for copy in frag_loads:
        copy.start()

    row = lax.broadcasted_iota(jnp.int32, (OWN, EXT), 0)
    lane = lax.broadcasted_iota(jnp.int32, (OWN, EXT), 1)
    digits = jnp.zeros((OWN, EXT), jnp.int32)
    for i in range(OWN):
        target = targets_ref[i]
        digits = jnp.where(row == i, jnp.where(lane == 0, target >> 8, target & 255), digits)
    g_buf[xh, y, z, :, 4 * CHUNK : 4 * CHUNK + EXT] = digits.astype(F32).astype(BF16)
    pl.semaphore_wait(barrier, len(partners))

    def columns(c):
        return pl.ds(c * CHUNK, CHUNK + (EXT if c == 3 else 0))

    load.wait()

    def swap_x(c):
        block = g_buf.at[xh, y, z, :, columns(c)]
        return go([remote(block, block, x_sem.at[c], dev(dx=1))])

    def gather_a(h, c):
        block = g_buf.at[h, y, z, :, columns(c)]
        return [remote(block, block, a_sem.at[h, c, d - 1], dev_a(c // 2, d)) for d in (1, 2, 3)]

    def gather_b1(h, c):
        g = c // 2
        b = pos(g)[1]
        copies = [[None, None], [None, None]]
        for p in range(2):
            for i, d in enumerate((1, 3)):
                q = p if i == 0 else 1 - p
                block = g_buf.at[(h, *at(g, slice(2 * q, 2 * q + 2), b), slice(None), columns(c))]
                (copies[i][q],) = go([remote(block, block, b1_sem.at[h, c, i, q], dev_b(g, d))])
        return copies

    def gather_b2(h, c, first):
        g = c // 2
        b = pos(g)[1]
        copies = []
        for i, d in enumerate((1, 3)):
            first[i][i].wait_recv()
            block = g_buf.at[(h, *at(g, slice(2 * i, 2 * i + 2), (b + 4 - d) % 4), slice(None), columns(c))]
            copies += go([remote(block, block, b2_sem.at[h, c, i], dev_b(g, d))])
        return copies + [first[0][1], first[1][0]]

    def forward(h, c, second):
        arrived(second)
        if h == 0:
            head_loads[c].wait()
        lo = c * CHUNK
        rows = g_buf[h, :, :, :, lo : lo + CHUNK].reshape(HALF, CHUNK)
        out = jnp.dot(rows, head[lo : lo + CHUNK, :], preferred_element_type=F32)
        if c == ORDER[0]:
            logits[h] = out
        else:
            logits[h] = logits[h] + out

    eye = lax.broadcasted_iota(jnp.int32, (128, 128), 0) == lax.broadcasted_iota(jnp.int32, (128, 128), 1)

    def to_lanes(ref, i):
        return jnp.sum(jnp.where(eye, ref[128 * i : 128 * (i + 1), :], 0.0), axis=0, keepdims=True)

    STEP = 32

    def target_columns(h, i):
        t = g_buf[h, i // 2, pl.ds((i % 2) * 2, 2), :, 4 * CHUNK : 4 * CHUNK + EXT]
        t = t.reshape(STEP, EXT).astype(F32)
        return (t[:, 0:1] * 256.0 + t[:, 1:2]).astype(jnp.int32) - base

    def softmax_local(h):
        @pl.loop(0, HALF // STEP)
        def _(i):
            rows = pl.ds(pl.multiple_of(i * STEP, STEP), STEP)
            values = logits[h, rows, :]
            target = target_columns(h, i)
            column = lax.broadcasted_iota(jnp.int32, (STEP, width), 1)
            top = jnp.max(values, axis=1, keepdims=True)
            shifted = jnp.exp(values - top)
            logits[h, rows, :] = shifted
            col_top[h, rows, :] = jnp.broadcast_to(top, (STEP, 128))
            col_sum[rows, :] = jnp.broadcast_to(jnp.sum(shifted, axis=1, keepdims=True), (STEP, 128))
            picked = jnp.sum(jnp.where(column == target, values, 0.0), axis=1, keepdims=True)
            col_pick[rows, :] = jnp.broadcast_to(picked, (STEP, 128))

    def stat_send(h, stage):
        if stage == 0:
            slot = st_plane.at[h, xh, y]
            copies = [remote(slot, slot, st_sem.at[h, dx * NY + dy - 1], dev(dx=dx, dy=dy)) for dx, dy in plane]
        else:
            slot = st_z.at[h, z]
            copies = [remote(slot, slot, st_sem.at[h, 6 + d], dev(dz=d)) for d in (1, 2, 3)]
        return go(copies)

    def stats_start(h):
        tile = [to_lanes(col_top.at[h], i) for i in range(2)]
        tile += [to_lanes(ref, i) for ref in (col_sum, col_pick) for i in range(2)]
        tile += [jnp.zeros((2, 128), F32)]
        st_plane[h, xh, y] = jnp.concatenate(tile, axis=0)
        return stat_send(h, 0)

    def combine(tiles):
        tops = [tile[0:2] for tile in tiles]
        top = functools.reduce(jnp.maximum, tops)
        total = sum(tile[2:4] * jnp.exp(tile[0:2] - top) for tile in tiles)
        picked = sum(tile[4:6] for tile in tiles)
        return jnp.concatenate([top, total, picked, jnp.zeros((2, 128), F32)], axis=0)

    def stats_next(h, copies):
        arrived(copies)
        st_z[h, z] = combine([st_plane[h, i, j] for i in range(NX) for j in range(NY)])
        return stat_send(h, 1)

    def stats_end(h, copies):
        arrived(copies)
        fin[h] = combine([st_z[h, i] for i in range(NZ)])

    def gradient_logits(h):
        row_count = NX * HALF
        for i in range(2):
            top = jnp.broadcast_to(fin[h, i : i + 1, :], (128, 128))
            total = jnp.broadcast_to(fin[h, 2 + i : 3 + i, :], (128, 128))
            top = jnp.sum(jnp.where(eye, top, 0.0), axis=1, keepdims=True)
            total = jnp.sum(jnp.where(eye, total, 0.0), axis=1, keepdims=True)
            scale = jnp.exp(col_top[h, 128 * i : 128 * (i + 1), :] - top) / (total * row_count)
            col_sum[128 * i : 128 * (i + 1), :] = scale

        @pl.loop(0, HALF // STEP)
        def _(i):
            rows = pl.ds(pl.multiple_of(i * STEP, STEP), STEP)
            target = target_columns(h, i)
            column = lax.broadcasted_iota(jnp.int32, (STEP, width), 1)
            scale = col_sum[rows, 0:1]
            onehot = jnp.where(column == target, 1.0 / row_count, 0.0)
            dl[h, rows, :] = (logits[h, rows, :] * scale - onehot).astype(BF16)

    def piece(k):
        h, c = k // 4, ORDER[k % 4]
        g = c // 2
        a, b = pos(g)
        return h, c, g, a, b

    def backward(k):
        h, c, g, a, b = piece(k)

        out = lax.dot_general(
            dl[h], head[c * CHUNK : (c + 1) * CHUNK, :], (((1,), (1,)), ((), ())), preferred_element_type=F32
        )
        part[k] = out.reshape(NY, NZ, OWN, CHUNK)

        def own(d, first):
            return part[(k, *at(g, slice(first, first + 2), (b + d) % 4))]

        send1[k, 0, 0:2] = own(2, 0).astype(BF16)
        send1[k, 1, 2:4] = own(2, 2).astype(BF16)
        copies = [[None, None], [None, None]]
        for p in range(2):
            if p == 1:
                send1[k, 0, 2:4] = own(1, 2).astype(BF16)
                send1[k, 1, 0:2] = own(3, 0).astype(BF16)
            for i, d in enumerate((1, 3)):
                q = p if i == 0 else 1 - p
                half = pl.ds(2 * q, 2)
                (copies[i][q],) = go(
                    [remote(send1.at[k, i, half], recv1.at[k, i, half], r1_sem.at[k, i, q], dev_b(g, d))]
                )
        return copies

    def reduce_b(k, first):
        h, c, g, a, b = piece(k)
        copies = []
        for i, d in enumerate((1, 3)):
            first[i][i].wait_recv()
            mine = part[(k, *at(g, slice(2 * i, 2 * i + 2), (b + d) % 4))]
            send2[k, i] = (mine + recv1[k, i, 2 * i : 2 * i + 2].astype(F32)).astype(BF16)
            copies += go([remote(send2.at[k, i], recv2.at[k, i], r2_sem.at[k, i], dev_b(g, d))])
        return copies + [first[0][1], first[1][0]]

    def reduce_a(k, second):
        h, c, g, a, b = piece(k)
        arrived(second)
        for i in range(2):
            mine = part[(k, *at(g, slice(2 * i, 2 * i + 2), b))]
            near = recv1[k, 1 - i, 2 * i : 2 * i + 2].astype(F32)
            summed[k, 2 * i : 2 * i + 2] = mine + near + recv2[k, i].astype(F32)
        return go(
            [
                remote(summed.at[k, (a + d) % 4], recv_a.at[k, d - 1], ra_sem.at[k, d - 1], dev_a(g, d))
                for d in (1, 2, 3)
            ]
        )

    def reduce_x(k, copies):
        h, c, g, a, b = piece(k)
        arrived(copies)
        send_x[k] = summed[k, a] + recv_a[k, 0] + recv_a[k, 1] + recv_a[k, 2]
        copy = remote(send_x.at[k], recv_x.at[k % 4], rx_sem.at[k % 4], dev(dx=1))

        @pl.when(xh != h)
        def _():
            copy.start()

    def finish():
        for k in range(8):
            h, c, g, a, b = piece(k)
            copy = remote(send_x.at[k], recv_x.at[k % 4], rx_sem.at[k % 4], dev(dx=1))

            @pl.when(xh != h)
            def _():
                copy.wait_send()

            @pl.when(xh == h)
            def _():
                copy.wait_recv()
                grad_ref[:, c * CHUNK : (c + 1) * CHUNK] = (send_x[k] + recv_x[k % 4]).astype(BF16)

    def fragment():
        for copy in frag_loads:
            copy.wait()
        rows = g_buf[:, :, :, :, 0:FRAG].reshape(NX * HALF, FRAG)
        turned = rows.astype(F32).T.astype(BF16)

        @pl.loop(0, width // TILE)
        def _(j):
            cols = pl.ds(pl.multiple_of(j * TILE, TILE), TILE)
            grad = sum(
                jnp.dot(turned[:, h * HALF : (h + 1) * HALF], dl[h, :, cols], preferred_element_type=F32)
                for h in range(NX)
            )
            local = head[0:FRAG, cols].astype(F32) - 1.0 * grad
            outer_value = fg[:, cols]
            pseudo = (outer_value - local + pe[:, cols]) / REPLICAS
            momentum = 0.9 * mo[:, cols] + pseudo
            mo[:, cols] = momentum
            fg[:, cols] = outer_value - 0.7 * (pseudo + 0.9 * momentum)

        stores = [
            pltpu.make_async_copy(fg, new_global_hbm, out_sem.at[0]),
            pltpu.make_async_copy(mo, new_momentum_hbm, out_sem.at[1]),
        ]
        for copy in stores:
            copy.start()
        return stores

    def loss():
        terms = sum(fin[h, 0:2, :] + jnp.log(fin[h, 2:4, :]) - fin[h, 4:6, :] for h in range(NX))
        loss_ref[0] = jnp.sum(terms) / (NX * HALF)

    C0, C1, C2, C3 = ORDER
    xs = {c: swap_x(c) for c in ORDER}
    go(gather_a(xh, C0) + gather_a(xh, C1))
    for c in (C0, C1): arrived(xs[c]); go(gather_a(1 - xh, c))
    b1 = {}
    b2 = {}
    for c in (C0, C1): arrived(gather_a(0, c)); b1[0, c] = gather_b1(0, c)
    go(gather_a(xh, C2) + gather_a(xh, C3))
    for c in (C2, C3): arrived(xs[c]); go(gather_a(1 - xh, c))
    for c in (C0, C1): b2[0, c] = gather_b2(0, c, b1[0, c])
    for c in (C2, C3): arrived(gather_a(0, c)); b1[0, c] = gather_b1(0, c)
    forward(0, C0, b2[0, C0])
    for c in (C0, C1): arrived(gather_a(1, c)); b1[1, c] = gather_b1(1, c)
    for c in (C2, C3): b2[0, c] = gather_b2(0, c, b1[0, c])
    forward(0, C1, b2[0, C1])
    for c in (C2, C3): arrived(gather_a(1, c)); b1[1, c] = gather_b1(1, c)
    for c in (C0, C1): b2[1, c] = gather_b2(1, c, b1[1, c])
    forward(0, C2, b2[0, C2])
    forward(0, C3, b2[0, C3])
    for c in (C2, C3): b2[1, c] = gather_b2(1, c, b1[1, c])
    softmax_local(0)
    s0 = stats_start(0)
    forward(1, C0, b2[1, C0])
    forward(1, C1, b2[1, C1])
    s0 = stats_next(0, s0)
    forward(1, C2, b2[1, C2])
    forward(1, C3, b2[1, C3])
    softmax_local(1)
    s1 = stats_start(1)
    stats_end(0, s0)
    gradient_logits(0)
    r = {}
    r[0] = backward(0)
    r[1] = backward(1)
    r[2] = backward(2)
    r[3] = backward(3)
    s1 = stats_next(1, s1)
    r[0] = reduce_b(0, r[0])
    r[1] = reduce_b(1, r[1])
    r[2] = reduce_b(2, r[2])
    r[3] = reduce_b(3, r[3])
    stats_end(1, s1)
    gradient_logits(1)
    r[4] = backward(4)
    r[0] = reduce_a(0, r[0])
    r[5] = backward(5)
    r[1] = reduce_a(1, r[1])
    r[6] = backward(6)
    r[2] = reduce_a(2, r[2])
    r[7] = backward(7)
    r[3] = reduce_a(3, r[3])
    r[4] = reduce_b(4, r[4])
    reduce_x(0, r[0])
    r[5] = reduce_b(5, r[5])
    reduce_x(1, r[1])
    r[6] = reduce_b(6, r[6])
    reduce_x(2, r[2])
    r[7] = reduce_b(7, r[7])
    reduce_x(3, r[3])
    r[4] = reduce_a(4, r[4])
    r[5] = reduce_a(5, r[5])
    r[6] = reduce_a(6, r[6])
    r[7] = reduce_a(7, r[7])
    stores = fragment()
    loss()
    reduce_x(4, r[4])
    reduce_x(5, r[5])
    reduce_x(6, r[6])
    reduce_x(7, r[7])
    finish()
    for copy in sent:
        copy.wait_send()
    for copy in stores:
        copy.wait()


def hand_over(loss_in, grad_in, global_in, momentum_in, loss_out, grad_out, global_out, momentum_out, grad, frag, sem):
    moves = [(grad_in, grad, grad_out)]
    step = FRAG // PARTS
    for i in range(PARTS):
        rows = pl.ds(i * step, step)
        for j, (src, dst) in enumerate(((global_in, global_out), (momentum_in, momentum_out))):
            moves.append((src.at[rows], frag.at[j, rows], dst.at[rows]))
    reads = [pltpu.make_async_copy(src, held, sem.at[0, i]) for i, (src, held, _) in enumerate(moves)]
    writes = [pltpu.make_async_copy(held, dst, sem.at[1, i]) for i, (_, held, dst) in enumerate(moves)]
    for read in reads:
        read.start()
    loss_out[0] = loss_in[0]
    for read, write in zip(reads, writes):
        read.wait()
        write.start()
    for write in writes:
        write.wait()


def body(hidden, targets, head, global_frag, momentum, peer_delta):
    own, depth = hidden.shape
    width = head.shape[1]
    dma = pltpu.SemaphoreType.DMA
    pieces = 8
    out_shape = (
        jax.ShapeDtypeStruct((1,), F32),
        jax.ShapeDtypeStruct((own, depth), BF16),
        jax.ShapeDtypeStruct((FRAG, width), F32),
        jax.ShapeDtypeStruct((FRAG, width), F32),
    )
    results = pl.pallas_call(
        kernel,
        out_shape=out_shape,
        in_specs=[pl.BlockSpec(memory_space=pltpu.SMEM)] + [pl.BlockSpec(memory_space=pl.ANY)] * 5,
        out_specs=(
            pl.BlockSpec(memory_space=pltpu.SMEM),
            pl.BlockSpec(memory_space=pltpu.VMEM),
            pl.BlockSpec(memory_space=pl.ANY),
            pl.BlockSpec(memory_space=pl.ANY),
        ),
        scratch_shapes=[
            pltpu.VMEM((depth, width), BF16),
            pltpu.VMEM((NX, NY, NZ, OWN, depth + EXT), BF16),
            pltpu.VMEM((NX, HALF, width), F32),
            pltpu.VMEM((NX, HALF, width), BF16),
            pltpu.VMEM((pieces, NY, NZ, OWN, CHUNK), F32),
            pltpu.VMEM((pieces, 2, 4, OWN, CHUNK), BF16),
            pltpu.VMEM((pieces, 2, 4, OWN, CHUNK), BF16),
            pltpu.VMEM((pieces, 2, 2, OWN, CHUNK), BF16),
            pltpu.VMEM((pieces, 2, 2, OWN, CHUNK), BF16),
            pltpu.VMEM((pieces, 4, OWN, CHUNK), F32),
            pltpu.VMEM((pieces, 3, OWN, CHUNK), F32),
            pltpu.VMEM((pieces, OWN, CHUNK), F32),
            pltpu.VMEM((4, OWN, CHUNK), F32),
            pltpu.VMEM((NX, NX, NY, 8, 128), F32),
            pltpu.VMEM((NX, NZ, 8, 128), F32),
            pltpu.VMEM((NX, 8, 128), F32),
            pltpu.VMEM((NX, HALF, 128), F32),
            pltpu.VMEM((HALF, 128), F32),
            pltpu.VMEM((HALF, 128), F32),
            pltpu.VMEM((FRAG, width), F32),
            pltpu.VMEM((FRAG, width), F32),
            pltpu.VMEM((FRAG, width), F32),
            dma(()),
            dma((4,)),
            dma((3,)),
            dma((2,)),
            dma((4, 2)),
            dma((2, 4, 3, 2)),
            dma((2, 4, 2, 2, 2)),
            dma((2, 4, 2, 2)),
            dma((2, 10, 2)),
            dma((pieces, 2, 2, 2)),
            dma((pieces, 2, 2)),
            dma((pieces, 3, 2)),
            dma((4, 2)),
        ],
        compiler_params=pltpu.CompilerParams(
            collective_id=0, has_side_effects=True, vmem_limit_bytes=62 << 20
        ),
        cost_estimate=pl.CostEstimate(flops=18 * 10**9, bytes_accessed=24 * 2**20, transcendentals=2**20),
    )(targets, hidden, head, global_frag, momentum, peer_delta)
    specs = (pl.BlockSpec(memory_space=pltpu.SMEM),) + (pl.BlockSpec(memory_space=pl.ANY),) * 3
    return pl.pallas_call(
        hand_over,
        out_shape=out_shape,
        in_specs=specs,
        out_specs=specs,
        scratch_shapes=[
            pltpu.VMEM((own, depth), BF16),
            pltpu.VMEM((2, FRAG, width), F32),
            dma((2, 1 + 2 * PARTS)),
        ],
    )(*results)


def solution(mesh):
    in_specs = (
        P(("outer", "vocab"), None),
        P(("outer", "vocab")),
        P("outer", "vocab"),
        P(None, "vocab"),
        P(None, "vocab"),
        P("outer", "vocab"),
    )
    out_specs = (P("outer"), P(("outer", "vocab"), None), P("outer", "vocab"), P("outer", "vocab"))
    return jax.shard_map(body, mesh=mesh, in_specs=in_specs, out_specs=out_specs, check_vma=False)
```

```python
import functools

import jax
import jax.numpy as jnp
from jax import lax
from jax.experimental import pallas as pl
from jax.experimental.pallas import tpu as pltpu
from jax.sharding import PartitionSpec as P

FRAG = 128
REPLICAS = 4
MESH = pl.DeviceIdType.MESH
F32, BF16 = jnp.float32, jnp.bfloat16

NY, NZ, NX = 4, 4, 2
OWN = 16
HALF = NY * NZ * OWN
CHUNK = 1024
EXT = 128
TILE = 512
PARTS = 1
ORDER = (0, 2, 1, 3)


def kernel(
    targets_ref, hidden_hbm, head_hbm, global_hbm, momentum_hbm, peer_hbm,
    loss_ref, grad_ref, new_global_hbm, new_momentum_hbm,
    head, g_buf, logits, dl, part, send1, recv1, send2, recv2, summed, recv_a, send_x, recv_x,
    st_plane, st_z, fin, col_top, col_sum, col_pick, fg, mo, pe,
    load_sem, head_sem, frag_sem, out_sem, x_sem, a_sem, b1_sem, b2_sem, st_sem, r1_sem, r2_sem, ra_sem, rx_sem,
):
    outer = lax.axis_index("outer")
    me = lax.axis_index("vocab")
    y, z, xh = me // (NZ * NX), (me // NX) % NZ, me % NX
    width = head.shape[1]
    base = me * width

    def dev(dy=0, dz=0, dx=0):
        return (outer, ((y + dy) % NY) * (NZ * NX) + ((z + dz) % NZ) * NX + (xh + dx) % NX)

    def dev_a(g, d):
        return dev(dy=d) if g == 0 else dev(dz=d)

    def dev_b(g, d):
        return dev(dz=d) if g == 0 else dev(dy=d)

    def at(g, a, b):
        return (a, b) if g == 0 else (b, a)

    def pos(g):
        return (y, z) if g == 0 else (z, y)

    def remote(src, dst, sems, device):
        return pltpu.make_async_remote_copy(
            src_ref=src, dst_ref=dst, send_sem=sems.at[0], recv_sem=sems.at[1], device_id=device, device_id_type=MESH
        )

    sent = []

    def go(copies):
        for copy in copies:
            copy.start()
            sent.append(copy)
        return copies

    def arrived(copies):
        for copy in copies:
            copy.wait_recv()

    barrier = pltpu.get_barrier_semaphore()
    plane = [(dx, dy) for dx in range(NX) for dy in range(NY) if dx or dy]
    partners = [dev(dz=d) for d in (1, 2, 3)] + [dev(dx=dx, dy=dy) for dx, dy in plane]
    for partner in partners:
        pl.semaphore_signal(barrier, inc=1, device_id=partner, device_id_type=MESH)

    load = pltpu.make_async_copy(hidden_hbm, g_buf.at[xh, y, z, :, pl.ds(0, 4 * CHUNK)], load_sem)
    load.start()
    head_loads = {}
    for c in ORDER:
        rows = pl.ds(c * CHUNK, CHUNK)
        head_loads[c] = pltpu.make_async_copy(head_hbm.at[rows], head.at[rows], head_sem.at[c])
        head_loads[c].start()
    frag_loads = [
        pltpu.make_async_copy(src, dst, frag_sem.at[i])
        for i, (src, dst) in enumerate(((global_hbm, fg), (momentum_hbm, mo), (peer_hbm, pe)))
    ]
    for copy in frag_loads:
        copy.start()

    row = lax.broadcasted_iota(jnp.int32, (OWN, EXT), 0)
    lane = lax.broadcasted_iota(jnp.int32, (OWN, EXT), 1)
    digits = jnp.zeros((OWN, EXT), jnp.int32)
    for i in range(OWN):
        target = targets_ref[i]
        digits = jnp.where(row == i, jnp.where(lane == 0, target >> 8, target & 255), digits)
    g_buf[xh, y, z, :, 4 * CHUNK : 4 * CHUNK + EXT] = digits.astype(F32).astype(BF16)
    pl.semaphore_wait(barrier, len(partners))

    def columns(c):
        return pl.ds(c * CHUNK, CHUNK + (EXT if c == 3 else 0))

    load.wait()

    def swap_x(c):
        block = g_buf.at[xh, y, z, :, columns(c)]
        return go([remote(block, block, x_sem.at[c], dev(dx=1))])

    def gather_a(h, c):
        block = g_buf.at[h, y, z, :, columns(c)]
        return [remote(block, block, a_sem.at[h, c, d - 1], dev_a(c // 2, d)) for d in (1, 2, 3)]

    def gather_b1(h, c):
        g = c // 2
        b = pos(g)[1]
        copies = [[None, None], [None, None]]
        for p in range(2):
            for i, d in enumerate((1, 3)):
                q = p if i == 0 else 1 - p
                block = g_buf.at[(h, *at(g, slice(2 * q, 2 * q + 2), b), slice(None), columns(c))]
                (copies[i][q],) = go([remote(block, block, b1_sem.at[h, c, i, q], dev_b(g, d))])
        return copies

    def gather_b2(h, c, first):
        g = c // 2
        b = pos(g)[1]
        copies = []
        for i, d in enumerate((1, 3)):
            first[i][i].wait_recv()
            block = g_buf.at[(h, *at(g, slice(2 * i, 2 * i + 2), (b + 4 - d) % 4), slice(None), columns(c))]
            copies += go([remote(block, block, b2_sem.at[h, c, i], dev_b(g, d))])
        return copies + [first[0][1], first[1][0]]

    def forward(h, c, second):
        arrived(second)
        if h == 0:
            head_loads[c].wait()
        lo = c * CHUNK
        rows = g_buf[h, :, :, :, lo : lo + CHUNK].reshape(HALF, CHUNK)
        out = jnp.dot(rows, head[lo : lo + CHUNK, :], preferred_element_type=F32)
        if c == ORDER[0]:
            logits[h] = out
        else:
            logits[h] = logits[h] + out

    eye = lax.broadcasted_iota(jnp.int32, (128, 128), 0) == lax.broadcasted_iota(jnp.int32, (128, 128), 1)

    def to_lanes(ref, i):
        return jnp.sum(jnp.where(eye, ref[128 * i : 128 * (i + 1), :], 0.0), axis=0, keepdims=True)

    STEP = 32

    def target_columns(h, i):
        t = g_buf[h, i // 2, pl.ds((i % 2) * 2, 2), :, 4 * CHUNK : 4 * CHUNK + EXT]
        t = t.reshape(STEP, EXT).astype(F32)
        return (t[:, 0:1] * 256.0 + t[:, 1:2]).astype(jnp.int32) - base

    def softmax_local(h):
        @pl.loop(0, HALF // STEP, unroll=2)
        def _(i):
            rows = pl.ds(pl.multiple_of(i * STEP, STEP), STEP)
            values = logits[h, rows, :]
            target = target_columns(h, i)
            column = lax.broadcasted_iota(jnp.int32, (STEP, width), 1)
            top = jnp.max(values, axis=1, keepdims=True)
            shifted = jnp.exp(values - top)
            logits[h, rows, :] = shifted
            col_top[h, rows, :] = jnp.broadcast_to(top, (STEP, 128))
            col_sum[rows, :] = jnp.broadcast_to(jnp.sum(shifted, axis=1, keepdims=True), (STEP, 128))
            picked = jnp.sum(jnp.where(column == target, values, 0.0), axis=1, keepdims=True)
            col_pick[rows, :] = jnp.broadcast_to(picked, (STEP, 128))

    def stat_send(h, stage):
        if stage == 0:
            slot = st_plane.at[h, xh, y]
            copies = [remote(slot, slot, st_sem.at[h, dx * NY + dy - 1], dev(dx=dx, dy=dy)) for dx, dy in plane]
        else:
            slot = st_z.at[h, z]
            copies = [remote(slot, slot, st_sem.at[h, 6 + d], dev(dz=d)) for d in (1, 2, 3)]
        return go(copies)

    def stats_start(h):
        tile = [to_lanes(col_top.at[h], i) for i in range(2)]
        tile += [to_lanes(ref, i) for ref in (col_sum, col_pick) for i in range(2)]
        tile += [jnp.zeros((2, 128), F32)]
        st_plane[h, xh, y] = jnp.concatenate(tile, axis=0)
        return stat_send(h, 0)

    def combine(tiles):
        tops = [tile[0:2] for tile in tiles]
        top = functools.reduce(jnp.maximum, tops)
        total = sum(tile[2:4] * jnp.exp(tile[0:2] - top) for tile in tiles)
        picked = sum(tile[4:6] for tile in tiles)
        return jnp.concatenate([top, total, picked, jnp.zeros((2, 128), F32)], axis=0)

    def stats_next(h, copies):
        arrived(copies)
        st_z[h, z] = combine([st_plane[h, i, j] for i in range(NX) for j in range(NY)])
        return stat_send(h, 1)

    def stats_end(h, copies):
        arrived(copies)
        fin[h] = combine([st_z[h, i] for i in range(NZ)])

    def gradient_logits(h):
        row_count = NX * HALF
        for i in range(2):
            top = jnp.broadcast_to(fin[h, i : i + 1, :], (128, 128))
            total = jnp.broadcast_to(fin[h, 2 + i : 3 + i, :], (128, 128))
            top = jnp.sum(jnp.where(eye, top, 0.0), axis=1, keepdims=True)
            total = jnp.sum(jnp.where(eye, total, 0.0), axis=1, keepdims=True)
            scale = jnp.exp(col_top[h, 128 * i : 128 * (i + 1), :] - top) / (total * row_count)
            col_sum[128 * i : 128 * (i + 1), :] = scale

        @pl.loop(0, HALF // STEP, unroll=2)
        def _(i):
            rows = pl.ds(pl.multiple_of(i * STEP, STEP), STEP)
            target = target_columns(h, i)
            column = lax.broadcasted_iota(jnp.int32, (STEP, width), 1)
            scale = col_sum[rows, 0:1]
            onehot = jnp.where(column == target, 1.0 / row_count, 0.0)
            dl[h, rows, :] = (logits[h, rows, :] * scale - onehot).astype(BF16)

    def piece(k):
        h, c = k // 4, ORDER[k % 4]
        g = c // 2
        a, b = pos(g)
        return h, c, g, a, b

    def backward(k):
        h, c, g, a, b = piece(k)

        out = lax.dot_general(
            dl[h], head[c * CHUNK : (c + 1) * CHUNK, :], (((1,), (1,)), ((), ())), preferred_element_type=F32
        )
        part[k] = out.reshape(NY, NZ, OWN, CHUNK)

        def own(d, first):
            return part[(k, *at(g, slice(first, first + 2), (b + d) % 4))]

        send1[k, 0, 0:2] = own(2, 0).astype(BF16)
        send1[k, 1, 2:4] = own(2, 2).astype(BF16)
        copies = [[None, None], [None, None]]
        for p in range(2):
            if p == 1:
                send1[k, 0, 2:4] = own(1, 2).astype(BF16)
                send1[k, 1, 0:2] = own(3, 0).astype(BF16)
            for i, d in enumerate((1, 3)):
                q = p if i == 0 else 1 - p
                half = pl.ds(2 * q, 2)
                (copies[i][q],) = go(
                    [remote(send1.at[k, i, half], recv1.at[k, i, half], r1_sem.at[k, i, q], dev_b(g, d))]
                )
        return copies

    def reduce_b(k, first):
        h, c, g, a, b = piece(k)
        copies = []
        for i, d in enumerate((1, 3)):
            first[i][i].wait_recv()
            mine = part[(k, *at(g, slice(2 * i, 2 * i + 2), (b + d) % 4))]
            send2[k, i] = (mine + recv1[k, i, 2 * i : 2 * i + 2].astype(F32)).astype(BF16)
            copies += go([remote(send2.at[k, i], recv2.at[k, i], r2_sem.at[k, i], dev_b(g, d))])
        return copies + [first[0][1], first[1][0]]

    def reduce_a(k, second):
        h, c, g, a, b = piece(k)
        arrived(second)
        for i in range(2):
            mine = part[(k, *at(g, slice(2 * i, 2 * i + 2), b))]
            near = recv1[k, 1 - i, 2 * i : 2 * i + 2].astype(F32)
            summed[k, 2 * i : 2 * i + 2] = mine + near + recv2[k, i].astype(F32)
        return go(
            [
                remote(summed.at[k, (a + d) % 4], recv_a.at[k, d - 1], ra_sem.at[k, d - 1], dev_a(g, d))
                for d in (1, 2, 3)
            ]
        )

    def reduce_x(k, copies):
        h, c, g, a, b = piece(k)
        arrived(copies)
        send_x[k] = summed[k, a] + recv_a[k, 0] + recv_a[k, 1] + recv_a[k, 2]
        copy = remote(send_x.at[k], recv_x.at[k % 4], rx_sem.at[k % 4], dev(dx=1))

        @pl.when(xh != h)
        def _():
            copy.start()

    def finish():
        for k in range(8):
            h, c, g, a, b = piece(k)
            copy = remote(send_x.at[k], recv_x.at[k % 4], rx_sem.at[k % 4], dev(dx=1))

            @pl.when(xh != h)
            def _():
                copy.wait_send()

            @pl.when(xh == h)
            def _():
                copy.wait_recv()
                grad_ref[:, c * CHUNK : (c + 1) * CHUNK] = (send_x[k] + recv_x[k % 4]).astype(BF16)

    def fragment():
        for copy in frag_loads:
            copy.wait()
        rows = g_buf[:, :, :, :, 0:FRAG].reshape(NX * HALF, FRAG)
        turned = rows.astype(F32).T.astype(BF16)

        @pl.loop(0, width // TILE)
        def _(j):
            cols = pl.ds(pl.multiple_of(j * TILE, TILE), TILE)
            grad = sum(
                jnp.dot(turned[:, h * HALF : (h + 1) * HALF], dl[h, :, cols], preferred_element_type=F32)
                for h in range(NX)
            )
            local = head[0:FRAG, cols].astype(F32) - 1.0 * grad
            outer_value = fg[:, cols]
            pseudo = (outer_value - local + pe[:, cols]) / REPLICAS
            momentum = 0.9 * mo[:, cols] + pseudo
            mo[:, cols] = momentum
            fg[:, cols] = outer_value - 0.7 * (pseudo + 0.9 * momentum)

        stores = [
            pltpu.make_async_copy(fg, new_global_hbm, out_sem.at[0]),
            pltpu.make_async_copy(mo, new_momentum_hbm, out_sem.at[1]),
        ]
        for copy in stores:
            copy.start()
        return stores

    def loss():
        terms = sum(fin[h, 0:2, :] + jnp.log(fin[h, 2:4, :]) - fin[h, 4:6, :] for h in range(NX))
        loss_ref[0] = jnp.sum(terms) / (NX * HALF)

    C0, C1, C2, C3 = ORDER
    xs = {c: swap_x(c) for c in ORDER}
    go(gather_a(xh, C0) + gather_a(xh, C1))
    for c in (C0, C1): arrived(xs[c]); go(gather_a(1 - xh, c))
    b1 = {}
    b2 = {}
    for c in (C0, C1): arrived(gather_a(0, c)); b1[0, c] = gather_b1(0, c)
    go(gather_a(xh, C2) + gather_a(xh, C3))
    for c in (C2, C3): arrived(xs[c]); go(gather_a(1 - xh, c))
    for c in (C0, C1): b2[0, c] = gather_b2(0, c, b1[0, c])
    for c in (C2, C3): arrived(gather_a(0, c)); b1[0, c] = gather_b1(0, c)
    forward(0, C0, b2[0, C0])
    for c in (C0, C1): arrived(gather_a(1, c)); b1[1, c] = gather_b1(1, c)
    for c in (C2, C3): b2[0, c] = gather_b2(0, c, b1[0, c])
    forward(0, C1, b2[0, C1])
    for c in (C2, C3): arrived(gather_a(1, c)); b1[1, c] = gather_b1(1, c)
    for c in (C0, C1): b2[1, c] = gather_b2(1, c, b1[1, c])
    forward(0, C2, b2[0, C2])
    forward(0, C3, b2[0, C3])
    for c in (C2, C3): b2[1, c] = gather_b2(1, c, b1[1, c])
    softmax_local(0)
    s0 = stats_start(0)
    forward(1, C0, b2[1, C0])
    forward(1, C1, b2[1, C1])
    s0 = stats_next(0, s0)
    forward(1, C2, b2[1, C2])
    forward(1, C3, b2[1, C3])
    softmax_local(1)
    s1 = stats_start(1)
    stats_end(0, s0)
    gradient_logits(0)
    r = {}
    r[0] = backward(0)
    r[1] = backward(1)
    r[2] = backward(2)
    r[3] = backward(3)
    s1 = stats_next(1, s1)
    r[0] = reduce_b(0, r[0])
    r[1] = reduce_b(1, r[1])
    r[2] = reduce_b(2, r[2])
    r[3] = reduce_b(3, r[3])
    stats_end(1, s1)
    gradient_logits(1)
    r[4] = backward(4)
    r[0] = reduce_a(0, r[0])
    r[5] = backward(5)
    r[1] = reduce_a(1, r[1])
    r[6] = backward(6)
    r[2] = reduce_a(2, r[2])
    r[7] = backward(7)
    r[3] = reduce_a(3, r[3])
    r[4] = reduce_b(4, r[4])
    reduce_x(0, r[0])
    r[5] = reduce_b(5, r[5])
    reduce_x(1, r[1])
    r[6] = reduce_b(6, r[6])
    reduce_x(2, r[2])
    r[7] = reduce_b(7, r[7])
    reduce_x(3, r[3])
    r[4] = reduce_a(4, r[4])
    r[5] = reduce_a(5, r[5])
    r[6] = reduce_a(6, r[6])
    r[7] = reduce_a(7, r[7])
    stores = fragment()
    loss()
    reduce_x(4, r[4])
    reduce_x(5, r[5])
    reduce_x(6, r[6])
    reduce_x(7, r[7])
    finish()
    for copy in sent:
        copy.wait_send()
    for copy in stores:
        copy.wait()


def hand_over(loss_in, grad_in, global_in, momentum_in, loss_out, grad_out, global_out, momentum_out, grad, frag, sem):
    moves = [(grad_in, grad, grad_out)]
    step = FRAG // PARTS
    for i in range(PARTS):
        rows = pl.ds(i * step, step)
        for j, (src, dst) in enumerate(((global_in, global_out), (momentum_in, momentum_out))):
            moves.append((src.at[rows], frag.at[j, rows], dst.at[rows]))
    reads = [pltpu.make_async_copy(src, held, sem.at[0, i]) for i, (src, held, _) in enumerate(moves)]
    writes = [pltpu.make_async_copy(held, dst, sem.at[1, i]) for i, (_, held, dst) in enumerate(moves)]
    for read in reads:
        read.start()
    loss_out[0] = loss_in[0]
    for read, write in zip(reads, writes):
        read.wait()
        write.start()
    for write in writes:
        write.wait()


def body(hidden, targets, head, global_frag, momentum, peer_delta):
    own, depth = hidden.shape
    width = head.shape[1]
    dma = pltpu.SemaphoreType.DMA
    pieces = 8
    out_shape = (
        jax.ShapeDtypeStruct((1,), F32),
        jax.ShapeDtypeStruct((own, depth), BF16),
        jax.ShapeDtypeStruct((FRAG, width), F32),
        jax.ShapeDtypeStruct((FRAG, width), F32),
    )
    results = pl.pallas_call(
        kernel,
        out_shape=out_shape,
        in_specs=[pl.BlockSpec(memory_space=pltpu.SMEM)] + [pl.BlockSpec(memory_space=pl.ANY)] * 5,
        out_specs=(
            pl.BlockSpec(memory_space=pltpu.SMEM),
            pl.BlockSpec(memory_space=pltpu.VMEM),
            pl.BlockSpec(memory_space=pl.ANY),
            pl.BlockSpec(memory_space=pl.ANY),
        ),
        scratch_shapes=[
            pltpu.VMEM((depth, width), BF16),
            pltpu.VMEM((NX, NY, NZ, OWN, depth + EXT), BF16),
            pltpu.VMEM((NX, HALF, width), F32),
            pltpu.VMEM((NX, HALF, width), BF16),
            pltpu.VMEM((pieces, NY, NZ, OWN, CHUNK), F32),
            pltpu.VMEM((pieces, 2, 4, OWN, CHUNK), BF16),
            pltpu.VMEM((pieces, 2, 4, OWN, CHUNK), BF16),
            pltpu.VMEM((pieces, 2, 2, OWN, CHUNK), BF16),
            pltpu.VMEM((pieces, 2, 2, OWN, CHUNK), BF16),
            pltpu.VMEM((pieces, 4, OWN, CHUNK), F32),
            pltpu.VMEM((pieces, 3, OWN, CHUNK), F32),
            pltpu.VMEM((pieces, OWN, CHUNK), F32),
            pltpu.VMEM((4, OWN, CHUNK), F32),
            pltpu.VMEM((NX, NX, NY, 8, 128), F32),
            pltpu.VMEM((NX, NZ, 8, 128), F32),
            pltpu.VMEM((NX, 8, 128), F32),
            pltpu.VMEM((NX, HALF, 128), F32),
            pltpu.VMEM((HALF, 128), F32),
            pltpu.VMEM((HALF, 128), F32),
            pltpu.VMEM((FRAG, width), F32),
            pltpu.VMEM((FRAG, width), F32),
            pltpu.VMEM((FRAG, width), F32),
            dma(()),
            dma((4,)),
            dma((3,)),
            dma((2,)),
            dma((4, 2)),
            dma((2, 4, 3, 2)),
            dma((2, 4, 2, 2, 2)),
            dma((2, 4, 2, 2)),
            dma((2, 10, 2)),
            dma((pieces, 2, 2, 2)),
            dma((pieces, 2, 2)),
            dma((pieces, 3, 2)),
            dma((4, 2)),
        ],
        compiler_params=pltpu.CompilerParams(
            collective_id=0, has_side_effects=True, vmem_limit_bytes=62 << 20
        ),
        cost_estimate=pl.CostEstimate(flops=18 * 10**9, bytes_accessed=24 * 2**20, transcendentals=2**20),
    )(targets, hidden, head, global_frag, momentum, peer_delta)
    specs = (pl.BlockSpec(memory_space=pltpu.SMEM),) + (pl.BlockSpec(memory_space=pl.ANY),) * 3
    return pl.pallas_call(
        hand_over,
        out_shape=out_shape,
        in_specs=specs,
        out_specs=specs,
        scratch_shapes=[
            pltpu.VMEM((own, depth), BF16),
            pltpu.VMEM((2, FRAG, width), F32),
            dma((2, 1 + 2 * PARTS)),
        ],
    )(*results)


def solution(mesh):
    in_specs = (
        P(("outer", "vocab"), None),
        P(("outer", "vocab")),
        P("outer", "vocab"),
        P(None, "vocab"),
        P(None, "vocab"),
        P("outer", "vocab"),
    )
    out_specs = (P("outer"), P(("outer", "vocab"), None), P("outer", "vocab"), P("outer", "vocab"))
    return jax.shard_map(body, mesh=mesh, in_specs=in_specs, out_specs=out_specs, check_vma=False)
```
